32 devices in a mesh: fsdp: 8 (over z, x), sp: 4 (over y, core).
Axes of the slice: x: 2, y: 2, z: 4, core: 2. Of those that a mesh axis runs over, the one named last changes fastest.
Arguments:
- tokens: bfloat16 [8, 512, 5120], P('fsdp', 'sp'), may hold values from -32 to 32
- w_query: bfloat16 [5120, 2560], P('fsdp', 'sp'), may hold values from -1 to 1
- w_key: bfloat16 [5120, 2560], P('fsdp', 'sp'), may hold values from -1 to 1
- values: bfloat16 [8, 512, 2560], P('fsdp', 'sp'), may hold values from -6 to 6
- grad_out: bfloat16 [8, 512, 2560], P('fsdp', 'sp'), may hold values from -6 to 6
- kv_index: int32 [8, 20, 4, 4], P('fsdp', 'sp'), may hold values from 0 to 3, as said below
- kv_count: int32 [8, 20, 4], P('fsdp', 'sp'), may hold values from 1 to 4, as said below
Outputs:
- grad_tokens: bfloat16 [8, 512, 5120], P('fsdp', 'sp')
- grad_values: bfloat16 [8, 512, 2560], P('fsdp', 'sp')
- grad_wq: float32 [5120, 2560], P('fsdp', 'sp')
- grad_wk: float32 [5120, 2560], P('fsdp', 'sp')
The draws below stay inside these ranges and needn't reach their ends.
Inputs may be any that keep to these rules, and one draw needn't show every extreme that they name: Each row kv_index[b, h, i, :] is a permutation of 0 to 3 whose first entry is i. Only the first kv_count[b, h, i] entries of row kv_index[b, h, i, :] are live; the rest are ignored.
All inputs are finite; a program needn't handle non-finite values.
Results may differ from the reference program's by a relative error of at most 0.015.
The reference program's roundings to bfloat16 on the way count: a program that leaves them out, or rounds other values in their place, can miss the bound.
Values may be sent and summed in bfloat16 or wider, within the bound.
A program may use at most 128 MiB of HBM per device.

```python
import math
import jax
import jax.numpy as jnp
from jax import lax

D = 5120
HEADS = 20
HEAD_DIM = 128
BLOCK = 128
LENGTH = 512
SAMPLES = 8
INNER = 2560


def draw_tokens(key, part):
    key_base, key_spike = jax.random.split(key, 2)
    drawn = jnp.clip(jax.random.normal(key_base, (SAMPLES, LENGTH, D), jnp.float32), -5.0, 5.0)
    block_width = D // SAMPLES
    owners = jax.random.permutation(key_spike, SAMPLES)
    column_block = jnp.arange(D, dtype=jnp.int32) // block_width
    boosted = jnp.where(column_block[None, :] == owners[:, None], 3.0, 1.0)
    drawn = drawn * boosted[:, None, :]
    return drawn.astype(jnp.bfloat16)


def weight_pair(key):
    key_one, key_two = jax.random.split(jax.random.fold_in(key, 71))
    first = jnp.clip(jax.random.normal(key_one, (D, HEADS * HEAD_DIM), jnp.float32), -5.0, 5.0)
    second = jnp.clip(jax.random.normal(key_two, (D, HEADS * HEAD_DIM), jnp.float32), -5.0, 5.0)
    return (first, second)


def draw_w_query(key, part):
    first, second = weight_pair(key)
    return (first / math.sqrt(D)).astype(jnp.bfloat16)


def draw_w_key(key, part):
    first, second = weight_pair(key)
    mixed = second
    return (mixed / math.sqrt(D)).astype(jnp.bfloat16)


def block_tables(key):
    key_rank, key_dense, key_count, key_head = jax.random.split(jax.random.fold_in(key, 29), 4)
    nblocks = LENGTH // BLOCK
    query_block = jnp.arange(nblocks, dtype=jnp.int32)[:, None]
    key_block = jnp.arange(nblocks, dtype=jnp.int32)[None, :]
    jitter_rank = jax.random.randint(key_rank, (SAMPLES, HEADS, nblocks, nblocks), 0, 2 * nblocks)
    distance = jnp.abs(query_block - key_block)
    ranking = (distance + jitter_rank) * nblocks + key_block
    ranking = jnp.where(query_block == key_block, -1, ranking)
    ordered = jnp.argsort(ranking, axis=-1, stable=True).astype(jnp.int32)
    density = jax.random.randint(key_dense, (SAMPLES, HEADS, 1), 1, nblocks + 1)
    counts = jax.random.randint(key_count, (SAMPLES, HEADS, nblocks), 1, density + 1)
    full_head = jax.random.randint(key_head, (SAMPLES, 1, 1), 0, HEADS)
    head_ids = jnp.arange(HEADS, dtype=jnp.int32)[None, :, None]
    counts = jnp.where(head_ids == full_head, nblocks, counts)
    return (ordered, counts.astype(jnp.int32))


def draw_kv_index(key, part):
    ordered, counts = block_tables(key)
    return ordered


def draw_kv_count(key, part):
    ordered, counts = block_tables(key)
    return counts


def shard_levels(stream_key, dims, shards, least, top_value):
    level = 1.0
    for dim, shards_of in shards:
        heights = jax.random.uniform(jax.random.fold_in(jax.random.fold_in(stream_key, 6), dim), (shards_of,), jnp.float32, least / len(shards), top_value / len(shards))
        level = level * jnp.repeat(jnp.exp(heights), dims[dim] // shards_of).reshape((-1,) + (1,) * (len(dims) - 1 - dim))
    return level


def noise(key, dims, scale, bound, pieces=(), kind=jnp.bfloat16):
    factor_of = shard_levels(key, dims, pieces, -0.22, 0.18) if pieces else 1.0
    values = jax.random.normal(key, dims, jnp.float32) * scale * factor_of
    return jnp.minimum(jnp.maximum(values, -bound), bound).astype(kind)


def setup_inputs(seed: int = 0) -> dict:
    splits = jax.random.split(jax.random.key(seed), 8)
    return {
        "tokens": draw_tokens(jax.random.fold_in(splits[7], 71), 0),
        "w_query": draw_w_query(jax.random.fold_in(splits[7], 71), 0),
        "w_key": draw_w_key(jax.random.fold_in(splits[7], 71), 0),
        "values": noise(splits[3], (SAMPLES, LENGTH, INNER), 1.0, 6.0, ((0, 8), (1, 4))),
        "grad_out": noise(splits[4], (SAMPLES, LENGTH, INNER), 1.0, 6.0, ((0, 8), (1, 4))),
        "kv_index": draw_kv_index(jax.random.fold_in(splits[7], 71), 0),
        "kv_count": draw_kv_count(jax.random.fold_in(splits[7], 71), 0),
    }


def live_blocks(kv_index, kv_count):
    nblocks = kv_index.shape[-1]
    slot_ids = jnp.arange(nblocks, dtype=jnp.int32)
    in_use = slot_ids[None, None, :] < kv_count[:, :, None]
    matches = (kv_index[:, :, :, None] == slot_ids[None, None, None, :]) & in_use[:, :, :, None]
    return jnp.any(matches, axis=2)

def attend_back(query, keys, values, upstream, live):
    length = query.shape[0]
    count_heads = live.shape[0]
    scale = 1.0 / math.sqrt(HEAD_DIM)
    query_h = query.reshape(length, count_heads, HEAD_DIM).astype(jnp.float32)
    keys_h = keys.reshape(length, count_heads, HEAD_DIM).astype(jnp.float32)
    values_h = values.reshape(length, count_heads, HEAD_DIM).astype(jnp.float32)
    upstream_h = upstream.reshape(length, count_heads, HEAD_DIM).astype(jnp.float32)
    scores = jnp.einsum('qhd,khd->hqk', query_h, keys_h) * scale
    token_live = jnp.repeat(jnp.repeat(live, BLOCK, axis=1), BLOCK, axis=2)
    scores = jnp.where(token_live, scores, -jnp.inf)
    row_max = lax.optimization_barrier(jnp.max(scores, axis=2, keepdims=True))
    expon = jnp.exp(scores - row_max)
    probs = expon / lax.optimization_barrier(jnp.sum(expon, axis=2, keepdims=True))
    probs_low = probs.astype(jnp.bfloat16).astype(jnp.float32)
    dprob = jnp.einsum('qhd,khd->hqk', upstream_h, values_h)
    delta = lax.optimization_barrier(jnp.sum(probs * dprob, axis=2, keepdims=True))
    dscore = (probs * (dprob - delta) * scale).astype(jnp.bfloat16).astype(jnp.float32)
    grad_q = jnp.einsum('hqk,khd->qhd', dscore, keys_h).astype(jnp.bfloat16)
    grad_k = jnp.einsum('hqk,qhd->khd', dscore, query_h).astype(jnp.bfloat16)
    grad_v = jnp.einsum('hqk,qhd->khd', probs_low, upstream_h).astype(jnp.bfloat16)
    return (grad_q.reshape(length, -1), grad_k.reshape(length, -1), grad_v.reshape(length, -1))

def reference(tokens, w_query, w_key, values, grad_out, kv_index, kv_count):
    zeros_w = jnp.zeros(w_query.shape, jnp.float32)

    def one_sample(carry, items):
        sample_x, sample_v, sample_g, sample_index, sample_count = items
        query = jnp.dot(sample_x, w_query, preferred_element_type=jnp.float32).astype(jnp.bfloat16)
        keys = jnp.dot(sample_x, w_key, preferred_element_type=jnp.float32).astype(jnp.bfloat16)
        live = live_blocks(sample_index, sample_count)
        grad_q, grad_k, grad_v = attend_back(query, keys, sample_v, sample_g, live)
        grad_x = jnp.dot(grad_q, w_query.T, preferred_element_type=jnp.float32)
        grad_x = (grad_x + jnp.dot(grad_k, w_key.T, preferred_element_type=jnp.float32)).astype(jnp.bfloat16)
        term_q = jnp.dot(sample_x.T, grad_q, preferred_element_type=jnp.float32).astype(jnp.bfloat16)
        term_q = lax.optimization_barrier(term_q).astype(jnp.float32)
        term_k = jnp.dot(sample_x.T, grad_k, preferred_element_type=jnp.float32).astype(jnp.bfloat16)
        term_k = lax.optimization_barrier(term_k).astype(jnp.float32)
        return ((carry[0] + term_q, carry[1] + term_k), (grad_x, grad_v))
    sums, grads = lax.scan(one_sample, (zeros_w, zeros_w), (tokens, values, grad_out, kv_index, kv_count))
    return (grads[0], grads[1], sums[0], sums[1])
```

```python
import functools
import math

import jax
import jax.numpy as jnp
from jax import lax
from jax.experimental import pallas as pl
from jax.experimental.pallas import tpu as pltpu
from jax.sharding import PartitionSpec as P

HEAD_DIM = 128
PARTS = 4
BF16 = jnp.bfloat16
F32 = jnp.float32


def remote(src, dst, send_sem, recv_sem, axis, target):
    return pltpu.make_async_remote_copy(
        src_ref=src,
        dst_ref=dst,
        send_sem=send_sem,
        recv_sem=recv_sem,
        device_id={axis: target},
        device_id_type=pl.DeviceIdType.MESH,
    )


def place(n_f):
    f = lax.axis_index("fsdp")
    s = lax.axis_index("sp")
    return n_f // 2, f // 2, f % 2, s


def greet(n_f, n_s):
    depth, z, x, s = place(n_f)
    barrier = pltpu.get_barrier_semaphore()

    def signal(axis, target):
        pl.semaphore_signal(
            barrier, inc=1, device_id={axis: target}, device_id_type=pl.DeviceIdType.MESH
        )

    for k in range(1, n_s):
        signal("sp", (s + k) % n_s)
    signal("fsdp", z * 2 + 1 - x)

    @pl.when(z > 0)
    def _():
        signal("fsdp", (z - 1) * 2 + x)

    @pl.when(z < depth - 1)
    def _():
        signal("fsdp", (z + 1) * 2 + x)

    inner = (z > 0).astype(jnp.int32) + (z < depth - 1).astype(jnp.int32)
    pl.semaphore_wait(barrier, n_s + inner)


def gather_kernel(
    n_f, n_s, tok, wq, wk, val, gout, full_x, full_q, full_k, full_v, full_g, xt_out,
    x_in, xt, up_s, dn_s, x_s, z_r, x_r, sp_s, sp_r, loc, work,
):
    depth, z, x, s = place(n_f)
    rows = wq.shape[0]
    half = rows // 2
    t = tok.shape[0]
    hc = full_v.shape[1]
    ins, outs = (wq, wk), (full_q, full_k)

    def piece(zz, xx, c):
        start = (zz * 2 + xx) * rows + (c % 2) * half
        return outs[c // 2].at[pl.ds(pl.multiple_of(start, 16), half)]

    def own(c):
        return ins[c // 2].at[pl.ds((c % 2) * half, half)]

    def to_x(src, zz, c):
        return remote(src, piece(zz, x, c), x_s.at[zz, c], x_r.at[zz, c], "fsdp", z * 2 + 1 - x)

    def to_up(src, zz, c):
        return remote(src, piece(zz, x, c), up_s.at[zz, c], z_r.at[zz, c], "fsdp", (z + 1) * 2 + x)

    def to_dn(src, zz, c):
        return remote(src, piece(zz, x, c), dn_s.at[zz, c], z_r.at[zz, c], "fsdp", (z - 1) * 2 + x)

    def sp_copies(k):
        j = (s + k) % n_s
        mine = pl.ds(pl.multiple_of(s * t, 16), t)
        cols = pl.ds(pl.multiple_of(j * hc, 128), hc)
        return [
            remote(src, dst, sp_s.at[i, k - 1], sp_r.at[i, k - 1], "sp", j)
            for i, (src, dst) in enumerate(
                (
                    (tok, full_x.at[mine]),
                    (val.at[:, cols], full_v.at[mine]),
                    (gout.at[:, cols], full_g.at[mine]),
                )
            )
        ]

    mine = pl.ds(pl.multiple_of(s * t, 16), t)
    my_cols = pl.ds(pl.multiple_of(s * hc, 128), hc)
    my_rows = pl.ds(pl.multiple_of((z * 2 + x) * rows, 16), rows)
    locals_ = [
        pltpu.make_async_copy(src, dst, loc.at[i])
        for i, (src, dst) in enumerate(
            (
                (tok, full_x.at[mine]),
                (val.at[:, my_cols], full_v.at[mine]),
                (gout.at[:, my_cols], full_g.at[mine]),
                (wq, full_q.at[my_rows]),
                (wk, full_k.at[my_rows]),
            )
        )
    ]
    greet(n_f, n_s)
    for c in range(PARTS):
        to_x(own(c), z, c).start()

        @pl.when(z < depth - 1)
        def _():
            to_up(own(c), z, c).start()

        @pl.when(z > 0)
        def _():
            to_dn(own(c), z, c).start()

    for k in range(1, n_s):
        for copy in sp_copies(k):
            copy.start()
    for copy in locals_:
        copy.start()

    def forward(d):
        for c in range(PARTS):

            @pl.when(z - d >= 0)
            def _():
                zz = z - d
                blk = piece(zz, x, c)
                to_up(blk, zz, c).wait_recv()

                @pl.when(z < depth - 1)
                def _():
                    to_up(blk, zz, c).start()

                to_x(blk, zz, c).start()

            @pl.when(z + d < depth)
            def _():
                zz = z + d
                blk = piece(zz, x, c)
                to_dn(blk, zz, c).wait_recv()

                @pl.when(z > 0)
                def _():
                    to_dn(blk, zz, c).start()

                to_x(blk, zz, c).start()

    @pl.loop(1, depth)
    def _(d):
        forward(d)

    for k in range(1, n_s):
        for copy in sp_copies(k):
            copy.wait()
    for copy in locals_:
        copy.wait()
    load = pltpu.make_async_copy(full_x, x_in, work.at[0])
    load.start()
    load.wait()

    @pl.loop(0, x_in.shape[1] // 128)
    def _(i):
        at = pl.ds(pl.multiple_of(i * 128, 128), 128)
        xt[at, :] = x_in[:, at].T

    store = pltpu.make_async_copy(xt, xt_out, work.at[1])
    store.start()

    @pl.loop(0, depth)
    def _(zz):
        for c in range(PARTS):
            other = piece(zz, 1 - x, c)
            remote(
                other, other, x_s.at[zz, c], x_r.at[zz, c], "fsdp", z * 2 + 1 - x
            ).wait_recv()
            to_x(own(c), zz, c).wait_send()

            @pl.when((zz <= z) & (z < depth - 1))
            def _():
                to_up(own(c), zz, c).wait_send()

            @pl.when((zz >= z) & (z > 0))
            def _():
                to_dn(own(c), zz, c).wait_send()

    store.wait()


def attend_kernel(idx, cnt, x, wq, wk, v, g, grad, grad_v, p_s, d_s):
    h = pl.program_id(0)
    nb = idx.shape[2]
    block = x.shape[0] // nb
    scale = 1.0 / math.sqrt(HEAD_DIM)
    both = jnp.dot(
        x[...], jnp.concatenate([wq[...], wk[...]], axis=1), preferred_element_type=F32
    ).astype(BF16)
    q, k = both[:, :HEAD_DIM], both[:, HEAD_DIM:]
    vv, gg = v[...], g[...]
    nt = (((1,), (1,)), ((), ()))
    tn = (((0,), (0,)), ((), ()))
    col = lax.broadcasted_iota(jnp.int32, (block, nb * block), 1) // block
    for i in range(nb):
        live = jnp.zeros(col.shape, jnp.bool_)
        for n in range(nb):
            j = jnp.where(n < cnt[h, i], idx[h, i, n], -1)
            live = live | (col == j)
        at = slice(i * block, (i + 1) * block)
        scores = lax.dot_general(q[at], k, nt, preferred_element_type=F32) * scale
        scores = jnp.where(live, scores, -jnp.inf)
        expon = jnp.exp(scores - jnp.max(scores, axis=1, keepdims=True))
        probs = expon / jnp.sum(expon, axis=1, keepdims=True)
        dprob = lax.dot_general(gg[at], vv, nt, preferred_element_type=F32)
        delta = jnp.sum(probs * dprob, axis=1, keepdims=True)
        p_s[at, :] = probs.astype(BF16)
        d_s[at, :] = (probs * (dprob - delta) * scale).astype(BF16)
    d = d_s[...]
    grad[0] = jnp.dot(d, k, preferred_element_type=F32).astype(BF16)
    grad[1] = lax.dot_general(d, q, tn, preferred_element_type=F32).astype(BF16)
    grad_v[...] = lax.dot_general(p_s[...], gg, tn, preferred_element_type=F32).astype(BF16)


def scatter_kernel(
    n_f, n_s, chunk, xt_h, full_q, full_k, grad, gv, gx_out, gv_out, gw_out,
    xt, wbuf, xsend, xrecv, own, zrecv, gx, gxr,
    x_s, x_r, z_s, z_r, sp_s, sp_r, work,
):
    depth, z, x, s = place(n_f)
    rows, cols = gw_out.shape[1], gw_out.shape[2]
    half = rows // 2
    t, width = gx_out.shape

    def w_copy(i, slot):
        at = pl.ds(pl.multiple_of(i * chunk, 128), chunk)
        return [
            pltpu.make_async_copy(src.at[at], wbuf.at[slot, w], work.at[1 + w, slot])
            for w, src in enumerate((full_q, full_k))
        ]

    load = pltpu.make_async_copy(xt_h, xt, work.at[0, 0])
    load.start()
    for copy in w_copy(0, 0):
        copy.start()

    def order(i):
        odd = i % 2
        return odd * (i // 2) + (1 - odd) * (depth - 1 - i // 2)

    def part(c):
        w = c // 2
        return w, pl.ds(pl.multiple_of((c % 2) * half, 16), half)

    def term(zz, xx, c):
        start = (zz * 2 + xx) * rows + (c % 2) * half
        at = pl.ds(pl.multiple_of(start, 16), half)
        return jnp.dot(xt[at, :], grad[c // 2], preferred_element_type=F32).astype(BF16)

    def to_x(zz, c):
        w, at = part(c)
        return remote(
            xsend.at[zz, w, at], xrecv.at[zz, w, at], x_s.at[zz, c], x_r.at[zz, c],
            "fsdp", z * 2 + 1 - x,
        )

    def to_z(zz, c, slot, target):
        w, at = part(c)
        return remote(
            own.at[zz, w, at], zrecv.at[slot, w, at], z_s.at[zz, c], z_r.at[slot, c],
            "fsdp", target * 2 + x,
        )

    def gv_copy(k):
        j = (s + k) % n_s
        return remote(
            gv.at[pl.ds(pl.multiple_of(j * t, 16), t)],
            gv_out.at[:, pl.ds(pl.multiple_of(s * cols, 128), cols)],
            sp_s.at[0, k - 1], sp_r.at[0, k - 1], "sp", j,
        )

    def gx_copy(k):
        j = (s + k) % n_s
        return remote(
            gx.at[pl.ds(pl.multiple_of(j * t, 16), t)], gxr.at[k - 1],
            sp_s.at[1, k - 1], sp_r.at[1, k - 1], "sp", j,
        )

    gv_own = pltpu.make_async_copy(
        gv.at[pl.ds(pl.multiple_of(s * t, 16), t)],
        gv_out.at[:, pl.ds(pl.multiple_of(s * cols, 128), cols)],
        work.at[0, 1],
    )
    gv_own.start()
    greet(n_f, n_s)
    for k in range(1, n_s):
        gv_copy(k).start()
    load.wait()

    @pl.loop(0, depth * PARTS)
    def _(i):
        zz, c = order(i // PARTS), i % PARTS
        w, at = part(c)
        xsend[zz, w, at, :] = term(zz, 1 - x, c)
        to_x(zz, c).start()

    @pl.loop(0, depth * PARTS)
    def _(i):
        zz, c = i // PARTS, i % PARTS
        w, at = part(c)
        own[zz, w, at, :] = term(zz, x, c)

    nt = (((1,), (1,)), ((), ()))
    chunks = width // chunk

    @pl.loop(0, chunks)
    def _(i):
        slot = i % 2
        for copy in w_copy(i, slot):
            copy.wait()

        @pl.when(i + 1 < chunks)
        def _():
            for copy in w_copy(i + 1, 1 - slot):
                copy.start()

        acc = lax.dot_general(grad[0], wbuf[slot, 0], nt, preferred_element_type=F32)
        acc += lax.dot_general(grad[1], wbuf[slot, 1], nt, preferred_element_type=F32)
        gx[:, pl.ds(pl.multiple_of(i * chunk, 128), chunk)] = acc.astype(BF16)

    for k in range(1, n_s):
        gx_copy(k).start()

    @pl.loop(0, depth * PARTS)
    def _(i):
        zz, c = order(i // PARTS), i % PARTS
        w, at = part(c)
        to_x(zz, c).wait_recv()
        more = ((zz > z) & (z > 0)) | ((zz < z) & (z < depth - 1))

        def paired():
            return own[zz, w, at, :].astype(F32) + xrecv[zz, w, at, :].astype(F32)

        @pl.when(more)
        def _():
            to_z(zz, c, zz, z).wait_recv()
            own[zz, w, at, :] = (paired() + zrecv[zz, w, at, :].astype(F32)).astype(BF16)

        @pl.when(jnp.logical_not(more) & (zz != z))
        def _():
            own[zz, w, at, :] = paired().astype(BF16)

        @pl.when(zz > z)
        def _():
            to_z(zz, c, zz, z + 1).start()

        @pl.when(zz < z)
        def _():
            last = jnp.where(zz == z - 1, depth, zz)
            to_z(zz, c, last, z - 1).start()

        @pl.when(zz == z)
        def _():
            gw_out[w, at, :] = paired()

    for k in range(1, n_s):
        gx_copy(k).wait_recv()

    @pl.loop(0, chunks)
    def _(i):
        at = pl.ds(pl.multiple_of(i * chunk, 128), chunk)
        acc = gx[pl.ds(pl.multiple_of(s * t, 16), t), at].astype(F32)
        for k in range(n_s - 1):
            acc += gxr[k, :, at].astype(F32)
        gx_out[:, at] = acc.astype(BF16)

    @pl.loop(0, PARTS)
    def _(c):
        w, at = part(c)

        @pl.when(z > 0)
        def _():
            to_z(z, c, z, z).wait_recv()
            gw_out[w, at, :] += zrecv[z, w, at, :].astype(F32)

        @pl.when(z < depth - 1)
        def _():
            to_z(z, c, depth, z).wait_recv()
            gw_out[w, at, :] += zrecv[depth, w, at, :].astype(F32)

    @pl.loop(0, depth * PARTS)
    def _(i):
        zz, c = i // PARTS, i % PARTS
        to_x(zz, c).wait_send()

        @pl.when(zz != z)
        def _():
            to_z(zz, c, zz, z).wait_send()

    for k in range(1, n_s):
        gx_copy(k).wait_send()
        gv_copy(k).wait()
    gv_own.wait()


def local(n_f, n_s, tokens, w_query, w_key, values, grad_out, kv_index, kv_count):
    t, width = tokens.shape[1:]
    rows, cols = w_query.shape
    length = t * n_s
    heads = cols // HEAD_DIM
    depth = n_f // 2
    hbm = pl.BlockSpec(memory_space=pl.ANY)
    vmem = pl.BlockSpec(memory_space=pltpu.VMEM)
    smem = pl.BlockSpec(memory_space=pltpu.SMEM)
    dma = pltpu.SemaphoreType.DMA
    shape = jax.ShapeDtypeStruct
    full_x, full_q, full_k, full_v, full_g, xt = pl.pallas_call(
        functools.partial(gather_kernel, n_f, n_s),
        out_shape=(
            shape((length, width), BF16),
            shape((width, cols), BF16),
            shape((width, cols), BF16),
            shape((length, cols), BF16),
            shape((length, cols), BF16),
            shape((width, length), BF16),
        ),
        in_specs=[hbm] * 5,
        out_specs=(hbm,) * 6,
        scratch_shapes=[
            pltpu.VMEM((length, width), BF16),
            pltpu.VMEM((width, length), BF16),
            dma((depth, PARTS)),
            dma((depth, PARTS)),
            dma((depth, PARTS)),
            dma((depth, PARTS)),
            dma((depth, PARTS)),
            dma((3, n_s - 1)),
            dma((3, n_s - 1)),
            dma((5,)),
            dma((2,)),
        ],
        compiler_params=pltpu.CompilerParams(
            collective_id=0, has_side_effects=True, vmem_limit_bytes=60 * 2**20
        ),
        name="gather",
    )(tokens[0], w_query, w_key, values[0], grad_out[0])

    grad, gv = pl.pallas_call(
        attend_kernel,
        grid=(heads,),
        out_shape=(shape((2, length, cols), BF16), shape((length, cols), BF16)),
        in_specs=[
            smem,
            smem,
            pl.BlockSpec((length, width), lambda h: (0, 0)),
            pl.BlockSpec((width, HEAD_DIM), lambda h: (0, h)),
            pl.BlockSpec((width, HEAD_DIM), lambda h: (0, h)),
            pl.BlockSpec((length, HEAD_DIM), lambda h: (0, h)),
            pl.BlockSpec((length, HEAD_DIM), lambda h: (0, h)),
        ],
        out_specs=(
            pl.BlockSpec((2, length, HEAD_DIM), lambda h: (0, 0, h)),
            pl.BlockSpec((length, HEAD_DIM), lambda h: (0, h)),
        ),
        scratch_shapes=[pltpu.VMEM((length, length), BF16), pltpu.VMEM((length, length), BF16)],
        compiler_params=pltpu.CompilerParams(vmem_limit_bytes=60 * 2**20),
        name="attend",
    )(kv_index[0], kv_count[0], full_x, full_q, full_k, full_v, full_g)

    chunk = 512 if width % 512 == 0 else 128
    gx, token_gv, gw = pl.pallas_call(
        functools.partial(scatter_kernel, n_f, n_s, chunk),
        out_shape=(
            shape((t, width), BF16),
            shape((t, cols * n_s), BF16),
            shape((2, rows, cols), F32),
        ),
        in_specs=[hbm, hbm, hbm, vmem, vmem],
        out_specs=(vmem, hbm, vmem),
        scratch_shapes=[
            pltpu.VMEM((width, length), BF16),
            pltpu.VMEM((2, 2, chunk, cols), BF16),
            pltpu.VMEM((depth, 2, rows, cols), BF16),
            pltpu.VMEM((depth, 2, rows, cols), BF16),
            pltpu.VMEM((depth, 2, rows, cols), BF16),
            pltpu.VMEM((depth + 1, 2, rows, cols), BF16),
            pltpu.VMEM((length, width), BF16),
            pltpu.VMEM((n_s - 1, t, width), BF16),
            dma((depth, PARTS)),
            dma((depth, PARTS)),
            dma((depth, PARTS)),
            dma((depth + 1, PARTS)),
            dma((2, n_s - 1)),
            dma((2, n_s - 1)),
            dma((3, 2)),
        ],
        compiler_params=pltpu.CompilerParams(
            collective_id=1, has_side_effects=True, vmem_limit_bytes=60 * 2**20
        ),
        name="scatter",
    )(xt, full_q, full_k, grad, gv)
    return (gx[None], token_gv[None], gw[0], gw[1])


def solution(mesh):
    in_specs = (
        P("fsdp", "sp", None),
        P("fsdp", "sp"),
        P("fsdp", "sp"),
        P("fsdp", "sp", None),
        P("fsdp", "sp", None),
        P("fsdp", "sp", None, None),
        P("fsdp", "sp", None),
    )
    out_specs = (P("fsdp", "sp", None), P("fsdp", "sp", None), P("fsdp", "sp"), P("fsdp", "sp"))
    return jax.shard_map(
        functools.partial(local, mesh.shape["fsdp"], mesh.shape["sp"]),
        mesh=mesh,
        in_specs=in_specs,
        out_specs=out_specs,
        check_vma=False,
    )
```

```python
import functools
import math

import jax
import jax.numpy as jnp
from jax import lax
from jax.experimental import pallas as pl
from jax.experimental.pallas import tpu as pltpu
from jax.sharding import PartitionSpec as P

HEAD_DIM = 128
PARTS = 4
BF16 = jnp.bfloat16
F32 = jnp.float32


def remote(src, dst, send_sem, recv_sem, axis, target):
    return pltpu.make_async_remote_copy(
        src_ref=src,
        dst_ref=dst,
        send_sem=send_sem,
        recv_sem=recv_sem,
        device_id={axis: target},
        device_id_type=pl.DeviceIdType.MESH,
    )


def place(n_f):
    f = lax.axis_index("fsdp")
    s = lax.axis_index("sp")
    return n_f // 2, f // 2, f % 2, s


def greet(n_f, n_s):
    depth, z, x, s = place(n_f)
    barrier = pltpu.get_barrier_semaphore()

    def signal(axis, target):
        pl.semaphore_signal(
            barrier, inc=1, device_id={axis: target}, device_id_type=pl.DeviceIdType.MESH
        )

    for k in range(1, n_s):
        signal("sp", (s + k) % n_s)
    signal("fsdp", z * 2 + 1 - x)

    @pl.when(z > 0)
    def _():
        signal("fsdp", (z - 1) * 2 + x)

    @pl.when(z < depth - 1)
    def _():
        signal("fsdp", (z + 1) * 2 + x)

    inner = (z > 0).astype(jnp.int32) + (z < depth - 1).astype(jnp.int32)
    pl.semaphore_wait(barrier, n_s + inner)


def first_rows(rows):
    return 32 * max(1, round(0.15 * rows / 32))


def gather_kernel(
    n_f, n_s, tok, wq, wk, val, gout, q_out, k_out, full_q, full_k, full_v, full_g, xt_out,
    x_in, xt, land, acc, up_s, dn_s, z_r, x_s, x_r, xf_s, xf_r, sp_s, sp_r, loc, out_sem, work,
):
    depth, z, x, s = place(n_f)
    rows = wq.shape[0]
    few = first_rows(rows)
    half = (rows - few) // 2
    t = tok.shape[0]
    hc = full_v.shape[1]
    ins = (wq, wk)
    spans = [(c // 2, few + (c % 2) * half, half) for c in range(PARTS)]
    early = [(w, 0, few) for w in range(2)]

    def span(p):
        return spans[p] if p < PARTS else early[(p - PARTS) % 2]

    def side(p):
        return 1 - x if p >= PARTS + 2 else x

    def piece(zz, xx, p):
        w, start, size = span(p)
        at = (zz * 2 + xx) * rows + start
        return land.at[w, pl.ds(pl.multiple_of(at, 16), size)]

    def own(p):
        w, start, size = span(p)
        return ins[w].at[pl.ds(start, size)]

    def to_x(src, zz, p):
        return remote(src, piece(zz, x, p), x_s.at[zz, p], x_r.at[zz, p], "fsdp", z * 2 + 1 - x)

    def early_x(w):
        return remote(
            own(PARTS + w), piece(z, x, PARTS + w), xf_s.at[w], xf_r.at[w], "fsdp", z * 2 + 1 - x
        )

    def to_z(src, zz, p, sems, step):
        return remote(
            src, piece(zz, side(p), p), sems.at[zz, p], z_r.at[zz, p], "fsdp", (z + step) * 2 + x
        )

    def send_z(src, zz, p, up, dn):
        if up:

            @pl.when(z < depth - 1)
            def _():
                to_z(src, zz, p, up_s, 1).start()

        if dn:

            @pl.when(z > 0)
            def _():
                to_z(src, zz, p, dn_s, -1).start()

    mine = pl.ds(pl.multiple_of(s * t, 16), t)
    my_cols = pl.ds(pl.multiple_of(s * hc, 128), hc)
    my_rows = pl.ds(pl.multiple_of((z * 2 + x) * rows, 16), rows)

    def sp_copies(k):
        j = (s + k) % n_s
        cols = pl.ds(pl.multiple_of(j * hc, 128), hc)
        return [
            remote(src, dst, sp_s.at[i, k - 1], sp_r.at[i, k - 1], "sp", j)
            for i, (src, dst) in enumerate(
                (
                    (tok, x_in.at[mine]),
                    (val.at[:, cols], full_v.at[mine]),
                    (gout.at[:, cols], full_g.at[mine]),
                )
            )
        ]

    locals_ = [
        pltpu.make_async_copy(src, dst, loc.at[i])
        for i, (src, dst) in enumerate(
            (
                (tok, x_in.at[mine]),
                (val.at[:, my_cols], full_v.at[mine]),
                (gout.at[:, my_cols], full_g.at[mine]),
                (wq, land.at[0, my_rows]),
                (wk, land.at[1, my_rows]),
            )
        )
    ]
    greet(n_f, n_s)
    for w in range(2):
        early_x(w).start()
    for p in range(PARTS):
        to_x(own(p), z, p).start()
        send_z(own(p), z, p, True, True)
    for w in range(2):
        send_z(own(PARTS + w), z, PARTS + w, True, True)
    for k in range(1, n_s):
        for copy in sp_copies(k):
            copy.start()
    for copy in locals_:
        copy.start()
    for w in range(2):
        other = piece(z, 1 - x, PARTS + 2 + w)
        remote(other, other, xf_s.at[w], xf_r.at[w], "fsdp", z * 2 + 1 - x).wait_recv()
        send_z(other, z, PARTS + 2 + w, True, True)
    acc[...] = jnp.zeros_like(acc)

    def both_ways(d, body):
        @pl.when(z - d >= 0)
        def _():
            body(z - d, True)

        @pl.when(z + d < depth)
        def _():
            body(z + d, False)

    def forward(d):
        for p in range(PARTS + 4):

            def body(zz, up):
                blk = piece(zz, side(p), p)
                to_z(blk, zz, p, up_s if up else dn_s, 0).wait_recv()
                send_z(blk, zz, p, up, not up)
                if p < PARTS:
                    to_x(blk, zz, p).start()

            both_ways(d, body)

    def keep(zz, xx, w):
        at = pl.ds(pl.multiple_of((zz * 2 + xx) * rows, 16), rows)
        return pltpu.make_async_copy(
            land.at[w, at], (full_q, full_k)[w].at[at], out_sem.at[zz * 2 + xx, w]
        )

    def project(zz, xx):
        at = pl.ds(pl.multiple_of((zz * 2 + xx) * rows, 16), rows)
        for w in range(2):
            keep(zz, xx, w).start()
            if rows % 128 == 0:
                cols = pl.ds(pl.multiple_of((zz * 2 + xx) * rows, 128), rows)
                acc[w] += jnp.dot(x_in[:, cols], land[w, at, :], preferred_element_type=F32)
            else:
                acc[w] += lax.dot_general(
                    xt[at, :], land[w, at, :], (((0,), (0,)), ((), ())), preferred_element_type=F32
                )

    def take_x(zz):
        for p in range(PARTS):
            other = piece(zz, 1 - x, p)
            remote(
                other, other, x_s.at[zz, p], x_r.at[zz, p], "fsdp", z * 2 + 1 - x
            ).wait_recv()
        project(zz, 1 - x)

    forward(1)
    for k in range(1, n_s):
        for copy in sp_copies(k):
            copy.wait()
    for copy in locals_:
        copy.wait()

    @pl.loop(0, x_in.shape[1] // 128)
    def _(i):
        at = pl.ds(pl.multiple_of(i * 128, 128), 128)
        xt[at, :] = x_in[:, at].T

    store = pltpu.make_async_copy(xt, xt_out, work.at[0])
    store.start()
    project(z, x)
    both_ways(1, lambda zz, up: project(zz, x))

    @pl.loop(2, depth)
    def _(d):
        forward(d)
        both_ways(d, lambda zz, up: project(zz, x))

        @pl.when(d == 2)
        def _():
            take_x(z)

        @pl.when(d > 2)
        def _():
            both_ways(d - 2, lambda zz, up: take_x(zz))

    if depth == 2:
        take_x(z)

    @pl.loop(max(1, depth - 2), depth)
    def _(d):
        both_ways(d, lambda zz, up: take_x(zz))

    q_out[...] = acc[0].astype(BF16)
    k_out[...] = acc[1].astype(BF16)

    for w in range(2):
        early_x(w).wait_send()

    @pl.loop(0, depth)
    def _(zz):
        for w in range(2):
            for xx in range(2):
                keep(zz, xx, w).wait()
        for p in range(PARTS):
            to_x(own(p), zz, p).wait_send()
        for p in range(PARTS + 4):

            @pl.when((zz <= z) & (z < depth - 1))
            def _():
                to_z(own(p), zz, p, up_s, 1).wait_send()

            @pl.when((zz >= z) & (z > 0))
            def _():
                to_z(own(p), zz, p, dn_s, -1).wait_send()

    store.wait()


def attend_kernel(live_bits, q_in, k_in, v, g, grad, grad_v, p_s, d_s):
    h = pl.program_id(0)
    nb = live_bits.shape[1]
    block = q_in.shape[0] // nb
    scale = 1.0 / math.sqrt(HEAD_DIM)
    q, k = q_in[...], k_in[...]
    vv, gg = v[...], g[...]
    nt = (((1,), (1,)), ((), ()))
    tn = (((0,), (0,)), ((), ()))
    col = lax.broadcasted_iota(jnp.int32, (block, nb * block), 1) // block
    for i in range(nb):
        live = ((live_bits[h, i] >> col) & 1) == 1
        at = slice(i * block, (i + 1) * block)
        scores = lax.dot_general(q[at], k, nt, preferred_element_type=F32) * scale
        scores = jnp.where(live, scores, -jnp.inf)
        expon = jnp.exp(scores - jnp.max(scores, axis=1, keepdims=True))
        probs = expon / jnp.sum(expon, axis=1, keepdims=True)
        dprob = lax.dot_general(gg[at], vv, nt, preferred_element_type=F32)
        delta = jnp.sum(probs * dprob, axis=1, keepdims=True)
        p_s[at, :] = probs.astype(BF16)
        d_s[at, :] = (probs * (dprob - delta) * scale).astype(BF16)
    d = d_s[...]
    grad[0] = jnp.dot(d, k, preferred_element_type=F32).astype(BF16)
    grad[1] = lax.dot_general(d, q, tn, preferred_element_type=F32).astype(BF16)
    grad_v[...] = lax.dot_general(p_s[...], gg, tn, preferred_element_type=F32).astype(BF16)


def scatter_kernel(
    n_f, n_s, chunk, xt_h, full_q, full_k, grad, gv, gx_out, gv_out, gw_out,
    xt, wbuf, xsend, xrecv, own, zrecv, fown, fzrecv, fxrecv, gx, gxr,
    x_s, x_r, z_s, z_r, fz_s, fz_r, fx_s, fx_r, sp_s, sp_r, work,
):
    depth, z, x, s = place(n_f)
    rows, cols = gw_out.shape[1], gw_out.shape[2]
    few = first_rows(rows)
    half = (rows - few) // 2
    t, width = gx_out.shape

    def w_copy(i, slot):
        at = pl.ds(pl.multiple_of(i * chunk, 128), chunk)
        return [
            pltpu.make_async_copy(src.at[at], wbuf.at[slot, w], work.at[1 + w, slot])
            for w, src in enumerate((full_q, full_k))
        ]

    load = pltpu.make_async_copy(xt_h, xt, work.at[0, 0])
    load.start()
    for copy in w_copy(0, 0):
        copy.start()

    def order(i):
        odd = i % 2
        return odd * (i // 2) + (1 - odd) * (depth - 1 - i // 2)

    def part(c):
        w = c // 2
        return w, pl.ds(pl.multiple_of((c % 2) * half, 16), half)

    def main_rows(c):
        return pl.ds(pl.multiple_of(few + (c % 2) * half, 16), half)

    def product(zz, xx, w, start, size):
        at = pl.ds(pl.multiple_of((zz * 2 + xx) * rows + start, 16), size)
        return jnp.dot(xt[at, :], grad[w], preferred_element_type=F32).astype(BF16)

    def term(zz, xx, c):
        return product(zz, xx, c // 2, few + (c % 2) * half, half)

    def early_z(zz, e, slot, target):
        return remote(
            fown.at[zz, e], fzrecv.at[slot, e], fz_s.at[zz, e], fz_r.at[slot, e],
            "fsdp", target * 2 + x,
        )

    def early_x(w):
        return remote(
            fown.at[z, 2 + w], fxrecv.at[w], fx_s.at[w], fx_r.at[w], "fsdp", z * 2 + 1 - x
        )

    def to_x(zz, c):
        w, at = part(c)
        return remote(
            xsend.at[zz, w, at], xrecv.at[zz, w, at], x_s.at[zz, c], x_r.at[zz, c],
            "fsdp", z * 2 + 1 - x,
        )

    def to_z(zz, c, slot, target):
        w, at = part(c)
        return remote(
            own.at[zz, w, at], zrecv.at[slot, w, at], z_s.at[zz, c], z_r.at[slot, c],
            "fsdp", target * 2 + x,
        )

    def gv_copy(k):
        j = (s + k) % n_s
        return remote(
            gv.at[pl.ds(pl.multiple_of(j * t, 16), t)],
            gv_out.at[:, pl.ds(pl.multiple_of(s * cols, 128), cols)],
            sp_s.at[0, k - 1], sp_r.at[0, k - 1], "sp", j,
        )

    def gx_copy(k):
        j = (s + k) % n_s
        return remote(
            gx.at[pl.ds(pl.multiple_of(j * t, 16), t)], gxr.at[k - 1],
            sp_s.at[1, k - 1], sp_r.at[1, k - 1], "sp", j,
        )

    gv_own = pltpu.make_async_copy(
        gv.at[pl.ds(pl.multiple_of(s * t, 16), t)],
        gv_out.at[:, pl.ds(pl.multiple_of(s * cols, 128), cols)],
        work.at[0, 1],
    )
    gv_own.start()
    greet(n_f, n_s)
    for k in range(1, n_s):
        gv_copy(k).start()
    load.wait()

    @pl.loop(0, depth * PARTS)
    def _(i):
        zz, c = order(i // PARTS), i % PARTS
        w, at = part(c)
        xsend[zz, w, at, :] = term(zz, 1 - x, c)
        to_x(zz, c).start()

    @pl.loop(0, depth * 4)
    def _(i):
        zz, e = order(i // 4), i % 4
        rel = e // 2
        fown[zz, e] = product(zz, x + rel * (1 - 2 * x), e % 2, 0, few)

        @pl.when((z == 0) & (zz > z))
        def _():
            early_z(zz, e, zz, z + 1).start()

        @pl.when((z == depth - 1) & (zz < z))
        def _():
            early_z(zz, e, jnp.where(zz == z - 1, depth, zz), z - 1).start()

    @pl.loop(0, depth * PARTS)
    def _(i):
        zz, c = i // PARTS, i % PARTS
        w, at = part(c)
        own[zz, w, at, :] = term(zz, x, c)

    @pl.loop(0, depth * 4)
    def _(i):
        zz, e = order(i // 4), i % 4
        more = ((zz > z) & (z > 0)) | ((zz < z) & (z < depth - 1))

        @pl.when(more)
        def _():
            early_z(zz, e, zz, z).wait_recv()
            fown[zz, e] = (fown[zz, e].astype(F32) + fzrecv[zz, e].astype(F32)).astype(BF16)

        @pl.when((z > 0) & (zz > z))
        def _():
            early_z(zz, e, zz, z + 1).start()

        @pl.when((z < depth - 1) & (zz < z))
        def _():
            early_z(zz, e, jnp.where(zz == z - 1, depth, zz), z - 1).start()

    nt = (((1,), (1,)), ((), ()))
    chunks = width // chunk

    @pl.loop(0, chunks)
    def _(i):
        slot = i % 2
        for copy in w_copy(i, slot):
            copy.wait()

        @pl.when(i + 1 < chunks)
        def _():
            for copy in w_copy(i + 1, 1 - slot):
                copy.start()

        acc = lax.dot_general(grad[0], wbuf[slot, 0], nt, preferred_element_type=F32)
        acc += lax.dot_general(grad[1], wbuf[slot, 1], nt, preferred_element_type=F32)
        gx[:, pl.ds(pl.multiple_of(i * chunk, 128), chunk)] = acc.astype(BF16)

    for k in range(1, n_s):
        gx_copy(k).start()

    def early_sum(e):
        @pl.when(z > 0)
        def _():
            early_z(z, e, z, z).wait_recv()

        @pl.when(z < depth - 1)
        def _():
            early_z(z, e, depth, z).wait_recv()

        below = jnp.where(z > 0, fzrecv[z, e].astype(F32), 0.0)
        above = jnp.where(z < depth - 1, fzrecv[depth, e].astype(F32), 0.0)
        return fown[z, e].astype(F32) + below + above

    for w in range(2):
        fown[z, 2 + w] = early_sum(2 + w).astype(BF16)
        early_x(w).start()
    for w in range(2):
        gw_out[w, :few, :] = early_sum(w)

    @pl.loop(0, depth * PARTS)
    def _(i):
        zz, c = order(i // PARTS), i % PARTS
        w, at = part(c)
        to_x(zz, c).wait_recv()
        more = ((zz > z) & (z > 0)) | ((zz < z) & (z < depth - 1))

        def paired():
            return own[zz, w, at, :].astype(F32) + xrecv[zz, w, at, :].astype(F32)

        @pl.when(more)
        def _():
            to_z(zz, c, zz, z).wait_recv()
            own[zz, w, at, :] = (paired() + zrecv[zz, w, at, :].astype(F32)).astype(BF16)

        @pl.when(jnp.logical_not(more) & (zz != z))
        def _():
            own[zz, w, at, :] = paired().astype(BF16)

        @pl.when(zz > z)
        def _():
            to_z(zz, c, zz, z + 1).start()

        @pl.when(zz < z)
        def _():
            last = jnp.where(zz == z - 1, depth, zz)
            to_z(zz, c, last, z - 1).start()

        @pl.when(zz == z)
        def _():
            gw_out[w, main_rows(c), :] = paired()

    for w in range(2):
        early_x(w).wait_recv()
        gw_out[w, :few, :] += fxrecv[w].astype(F32)

    for k in range(1, n_s):
        gx_copy(k).wait_recv()

    @pl.loop(0, chunks)
    def _(i):
        at = pl.ds(pl.multiple_of(i * chunk, 128), chunk)
        acc = gx[pl.ds(pl.multiple_of(s * t, 16), t), at].astype(F32)
        for k in range(n_s - 1):
            acc += gxr[k, :, at].astype(F32)
        gx_out[:, at] = acc.astype(BF16)

    @pl.loop(0, PARTS)
    def _(c):
        w, at = part(c)

        @pl.when(z > 0)
        def _():
            to_z(z, c, z, z).wait_recv()
            gw_out[w, main_rows(c), :] += zrecv[z, w, at, :].astype(F32)

        @pl.when(z < depth - 1)
        def _():
            to_z(z, c, depth, z).wait_recv()
            gw_out[w, main_rows(c), :] += zrecv[depth, w, at, :].astype(F32)

    @pl.loop(0, depth * PARTS)
    def _(i):
        zz, c = i // PARTS, i % PARTS
        to_x(zz, c).wait_send()

        @pl.when(zz != z)
        def _():
            to_z(zz, c, zz, z).wait_send()
            early_z(zz, c, zz, z).wait_send()

    for w in range(2):
        early_x(w).wait_send()

    for k in range(1, n_s):
        gx_copy(k).wait_send()
        gv_copy(k).wait()
    gv_own.wait()


def local(n_f, n_s, tokens, w_query, w_key, values, grad_out, kv_index, kv_count):
    t, width = tokens.shape[1:]
    rows, cols = w_query.shape
    length = t * n_s
    heads = cols // HEAD_DIM
    depth = n_f // 2
    hbm = pl.BlockSpec(memory_space=pl.ANY)
    vmem = pl.BlockSpec(memory_space=pltpu.VMEM)
    smem = pl.BlockSpec(memory_space=pltpu.SMEM)
    dma = pltpu.SemaphoreType.DMA
    shape = jax.ShapeDtypeStruct
    slots = PARTS + 4
    q, k, full_q, full_k, full_v, full_g, xt = pl.pallas_call(
        functools.partial(gather_kernel, n_f, n_s),
        out_shape=(
            shape((length, cols), BF16),
            shape((length, cols), BF16),
            shape((width, cols), BF16),
            shape((width, cols), BF16),
            shape((length, cols), BF16),
            shape((length, cols), BF16),
            shape((width, length), BF16),
        ),
        in_specs=[hbm] * 5,
        out_specs=(vmem, vmem) + (hbm,) * 5,
        scratch_shapes=[
            pltpu.VMEM((length, width), BF16),
            pltpu.VMEM((width, length), BF16),
            pltpu.VMEM((2, width, cols), BF16),
            pltpu.VMEM((2, length, cols), F32),
            dma((depth, slots)),
            dma((depth, slots)),
            dma((depth, slots)),
            dma((depth, PARTS)),
            dma((depth, PARTS)),
            dma((2,)),
            dma((2,)),
            dma((3, n_s - 1)),
            dma((3, n_s - 1)),
            dma((5,)),
            dma((n_f, 2)),
            dma((1,)),
        ],
        compiler_params=pltpu.CompilerParams(
            collective_id=0, has_side_effects=True, vmem_limit_bytes=60 * 2**20
        ),
        name="gather",
    )(tokens[0], w_query, w_key, values[0], grad_out[0])

    index, count = kv_index[0], kv_count[0]
    in_use = jnp.arange(index.shape[-1], dtype=jnp.int32) < count[..., None]
    live_bits = jnp.sum(jnp.where(in_use, 1 << index, 0), axis=-1, dtype=jnp.int32)
    head = pl.BlockSpec((length, HEAD_DIM), lambda h: (0, h))
    grad, gv = pl.pallas_call(
        attend_kernel,
        grid=(heads,),
        out_shape=(shape((2, length, cols), BF16), shape((length, cols), BF16)),
        in_specs=[smem, head, head, head, head],
        out_specs=(pl.BlockSpec((2, length, HEAD_DIM), lambda h: (0, 0, h)), head),
        scratch_shapes=[pltpu.VMEM((length, length), BF16), pltpu.VMEM((length, length), BF16)],
        compiler_params=pltpu.CompilerParams(vmem_limit_bytes=60 * 2**20),
        name="attend",
    )(live_bits, q, k, full_v, full_g)

    few = first_rows(rows)
    chunk = 512 if width % 512 == 0 else 128
    gx, token_gv, gw = pl.pallas_call(
        functools.partial(scatter_kernel, n_f, n_s, chunk),
        out_shape=(
            shape((t, width), BF16),
            shape((t, cols * n_s), BF16),
            shape((2, rows, cols), F32),
        ),
        in_specs=[hbm, hbm, hbm, vmem, vmem],
        out_specs=(vmem, hbm, vmem),
        scratch_shapes=[
            pltpu.VMEM((width, length), BF16),
            pltpu.VMEM((2, 2, chunk, cols), BF16),
            pltpu.VMEM((depth, 2, rows - few, cols), BF16),
            pltpu.VMEM((depth, 2, rows - few, cols), BF16),
            pltpu.VMEM((depth, 2, rows - few, cols), BF16),
            pltpu.VMEM((depth + 1, 2, rows - few, cols), BF16),
            pltpu.VMEM((depth, 4, few, cols), BF16),
            pltpu.VMEM((depth + 1, 4, few, cols), BF16),
            pltpu.VMEM((2, few, cols), BF16),
            pltpu.VMEM((length, width), BF16),
            pltpu.VMEM((n_s - 1, t, width), BF16),
            dma((depth, PARTS)),
            dma((depth, PARTS)),
            dma((depth, PARTS)),
            dma((depth + 1, PARTS)),
            dma((depth, 4)),
            dma((depth + 1, 4)),
            dma((2,)),
            dma((2,)),
            dma((2, n_s - 1)),
            dma((2, n_s - 1)),
            dma((3, 2)),
        ],
        compiler_params=pltpu.CompilerParams(
            collective_id=1, has_side_effects=True, vmem_limit_bytes=60 * 2**20
        ),
        name="scatter",
    )(xt, full_q, full_k, grad, gv)
    return (gx[None], token_gv[None], gw[0], gw[1])


def solution(mesh):
    in_specs = (
        P("fsdp", "sp", None),
        P("fsdp", "sp"),
        P("fsdp", "sp"),
        P("fsdp", "sp", None),
        P("fsdp", "sp", None),
        P("fsdp", "sp", None, None),
        P("fsdp", "sp", None),
    )
    out_specs = (P("fsdp", "sp", None), P("fsdp", "sp", None), P("fsdp", "sp"), P("fsdp", "sp"))
    return jax.shard_map(
        functools.partial(local, mesh.shape["fsdp"], mesh.shape["sp"]),
        mesh=mesh,
        in_specs=in_specs,
        out_specs=out_specs,
        check_vma=False,
    )
```

```python
import functools
import math

import jax
import jax.numpy as jnp
from jax import lax
from jax.experimental import pallas as pl
from jax.experimental.pallas import tpu as pltpu
from jax.sharding import PartitionSpec as P

HEAD_DIM = 128
PARTS = 4
BF16 = jnp.bfloat16
F32 = jnp.float32


def remote(src, dst, send_sem, recv_sem, axis, target):
    return pltpu.make_async_remote_copy(
        src_ref=src,
        dst_ref=dst,
        send_sem=send_sem,
        recv_sem=recv_sem,
        device_id={axis: target},
        device_id_type=pl.DeviceIdType.MESH,
    )


def place(n_f):
    f = lax.axis_index("fsdp")
    s = lax.axis_index("sp")
    return n_f // 2, f // 2, f % 2, s


def greet(n_f, n_s):
    depth, z, x, s = place(n_f)
    barrier = pltpu.get_barrier_semaphore()

    def signal(axis, target):
        pl.semaphore_signal(
            barrier, inc=1, device_id={axis: target}, device_id_type=pl.DeviceIdType.MESH
        )

    for k in range(1, n_s):
        signal("sp", (s + k) % n_s)
    signal("fsdp", z * 2 + 1 - x)

    @pl.when(z > 0)
    def _():
        signal("fsdp", (z - 1) * 2 + x)

    @pl.when(z < depth - 1)
    def _():
        signal("fsdp", (z + 1) * 2 + x)

    inner = (z > 0).astype(jnp.int32) + (z < depth - 1).astype(jnp.int32)
    pl.semaphore_wait(barrier, n_s + inner)


def first_rows(rows):
    return 32 * max(1, round(0.15 * rows / 32))


def gather_kernel(
    n_f, n_s, tok, wq, wk, val, gout, q_out, k_out, full_q, full_k, full_v, full_g, xt_out,
    x_in, xt, land, acc, up_s, dn_s, z_r, x_s, x_r, xf_s, xf_r, tok_s, tok_r, sp_s, sp_r, loc, out_sem, work,
):
    depth, z, x, s = place(n_f)
    rows = wq.shape[0]
    few = first_rows(rows)
    half = (rows - few) // 2
    t = tok.shape[0]
    hc = full_v.shape[1]
    ins = (wq, wk)
    spans = [(c // 2, few + (c % 2) * half, half) for c in range(PARTS)]
    early = [(w, 0, few) for w in range(2)]

    def span(p):
        return spans[p] if p < PARTS else early[(p - PARTS) % 2]

    def side(p):
        return 1 - x if p >= PARTS + 2 else x

    def piece(zz, xx, p):
        w, start, size = span(p)
        at = (zz * 2 + xx) * rows + start
        return land.at[w, pl.ds(pl.multiple_of(at, 16), size)]

    def own(p):
        w, start, size = span(p)
        return ins[w].at[pl.ds(start, size)]

    def to_x(src, zz, p):
        return remote(src, piece(zz, x, p), x_s.at[zz, p], x_r.at[zz, p], "fsdp", z * 2 + 1 - x)

    def early_x(w):
        return remote(
            own(PARTS + w), piece(z, x, PARTS + w), xf_s.at[w], xf_r.at[w], "fsdp", z * 2 + 1 - x
        )

    def to_z(src, zz, p, sems, step):
        return remote(
            src, piece(zz, side(p), p), sems.at[zz, p], z_r.at[zz, p], "fsdp", (z + step) * 2 + x
        )

    def send_z(src, zz, p, up, dn):
        if up:

            @pl.when(z < depth - 1)
            def _():
                to_z(src, zz, p, up_s, 1).start()

        if dn:

            @pl.when(z > 0)
            def _():
                to_z(src, zz, p, dn_s, -1).start()

    mine = pl.ds(pl.multiple_of(s * t, 16), t)
    my_cols = pl.ds(pl.multiple_of(s * hc, 128), hc)
    my_rows = pl.ds(pl.multiple_of((z * 2 + x) * rows, 16), rows)

    def sp_copies(k):
        j = (s + k) % n_s
        cols = pl.ds(pl.multiple_of(j * hc, 128), hc)
        return [
            remote(src, dst, sp_s.at[i, k - 1], sp_r.at[i, k - 1], "sp", j)
            for i, (src, dst) in enumerate(
                (
                    (val.at[:, cols], full_v.at[mine]),
                    (gout.at[:, cols], full_g.at[mine]),
                )
            )
        ]

    pairs, mate = n_s // 2, s + 1 - 2 * (s % 2)

    def tok_at(owner):
        return x_in.at[pl.ds(pl.multiple_of(owner * t, 16), t)]

    def friend(k):
        return ((s // 2 + k) % pairs) * 2 + s % 2

    def tok_direct(k):
        target = mate if k == 0 else friend(k)
        return remote(tok, tok_at(s), tok_s.at[k], tok_r.at[s], "sp", target)

    def tok_relay(owner, k):
        blk = tok_at(owner)
        return remote(blk, blk, tok_s.at[pairs - 1 + k], tok_r.at[owner], "sp", mate)

    locals_ = [
        pltpu.make_async_copy(src, dst, loc.at[i])
        for i, (src, dst) in enumerate(
            (
                (tok, x_in.at[mine]),
                (val.at[:, my_cols], full_v.at[mine]),
                (gout.at[:, my_cols], full_g.at[mine]),
                (wq, land.at[0, my_rows]),
                (wk, land.at[1, my_rows]),
            )
        )
    ]
    greet(n_f, n_s)
    for w in range(2):
        early_x(w).start()
    for p in range(PARTS):
        to_x(own(p), z, p).start()
        send_z(own(p), z, p, True, True)
    for w in range(2):
        send_z(own(PARTS + w), z, PARTS + w, True, True)
    for k in range(pairs):
        tok_direct(k).start()
    for k in range(1, n_s):
        for copy in sp_copies(k):
            copy.start()
    for copy in locals_:
        copy.start()
    for w in range(2):
        other = piece(z, 1 - x, PARTS + 2 + w)
        remote(other, other, xf_s.at[w], xf_r.at[w], "fsdp", z * 2 + 1 - x).wait_recv()
        send_z(other, z, PARTS + 2 + w, True, True)
    acc[...] = jnp.zeros_like(acc)

    def both_ways(d, body):
        @pl.when(z - d >= 0)
        def _():
            body(z - d, True)

        @pl.when(z + d < depth)
        def _():
            body(z + d, False)

    def forward(d):
        for p in range(PARTS + 4):

            def body(zz, up):
                blk = piece(zz, side(p), p)
                to_z(blk, zz, p, up_s if up else dn_s, 0).wait_recv()
                send_z(blk, zz, p, up, not up)
                if p < PARTS:
                    to_x(blk, zz, p).start()

            both_ways(d, body)

    def keep(zz, xx, w):
        at = pl.ds(pl.multiple_of((zz * 2 + xx) * rows, 16), rows)
        return pltpu.make_async_copy(
            land.at[w, at], (full_q, full_k)[w].at[at], out_sem.at[zz * 2 + xx, w]
        )

    def project(zz, xx):
        at = pl.ds(pl.multiple_of((zz * 2 + xx) * rows, 16), rows)
        for w in range(2):
            keep(zz, xx, w).start()
            if rows % 128 == 0:
                cols = pl.ds(pl.multiple_of((zz * 2 + xx) * rows, 128), rows)
                acc[w] += jnp.dot(x_in[:, cols], land[w, at, :], preferred_element_type=F32)
            else:
                acc[w] += lax.dot_general(
                    xt[at, :], land[w, at, :], (((0,), (0,)), ((), ())), preferred_element_type=F32
                )

    def take_x(zz):
        for p in range(PARTS):
            other = piece(zz, 1 - x, p)
            remote(
                other, other, x_s.at[zz, p], x_r.at[zz, p], "fsdp", z * 2 + 1 - x
            ).wait_recv()
        project(zz, 1 - x)

    forward(1)
    for k in range(1, pairs):
        tok_relay(friend(k), k).wait_recv()
        tok_relay(friend(k), k).start()
    for copy in locals_:
        copy.wait()
    for k in range(pairs):
        tok_relay(friend(k) + 1 - 2 * (s % 2), k).wait_recv()

    @pl.loop(0, x_in.shape[1] // 128)
    def _(i):
        at = pl.ds(pl.multiple_of(i * 128, 128), 128)
        xt[at, :] = x_in[:, at].T

    store = pltpu.make_async_copy(xt, xt_out, work.at[0])
    store.start()
    project(z, x)

    @pl.loop(2, depth)
    def _(d):
        forward(d)
        both_ways(d - 1, lambda zz, up: project(zz, x))

        @pl.when(d == 2)
        def _():
            take_x(z)

        @pl.when(d > 2)
        def _():
            both_ways(d - 2, lambda zz, up: take_x(zz))

    both_ways(depth - 1, lambda zz, up: project(zz, x))
    if depth == 2:
        take_x(z)

    @pl.loop(max(1, depth - 2), depth)
    def _(d):
        both_ways(d, lambda zz, up: take_x(zz))

    q_out[...] = acc[0].astype(BF16)
    k_out[...] = acc[1].astype(BF16)

    for k in range(1, n_s):
        for copy in sp_copies(k):
            copy.wait()
    for k in range(pairs):
        tok_direct(k).wait_send()
    for k in range(1, pairs):
        tok_relay(friend(k), k).wait_send()
    for w in range(2):
        early_x(w).wait_send()

    @pl.loop(0, depth)
    def _(zz):
        for w in range(2):
            for xx in range(2):
                keep(zz, xx, w).wait()
        for p in range(PARTS):
            to_x(own(p), zz, p).wait_send()
        for p in range(PARTS + 4):

            @pl.when((zz <= z) & (z < depth - 1))
            def _():
                to_z(own(p), zz, p, up_s, 1).wait_send()

            @pl.when((zz >= z) & (z > 0))
            def _():
                to_z(own(p), zz, p, dn_s, -1).wait_send()

    store.wait()


def attend_kernel(live_bits, q_in, k_in, v, g, grad, grad_v, p_s, d_s):
    h = pl.program_id(0)
    nb = live_bits.shape[1]
    block = q_in.shape[0] // nb
    scale = 1.0 / math.sqrt(HEAD_DIM)
    q, k = q_in[...], k_in[...]
    vv, gg = v[...], g[...]
    nt = (((1,), (1,)), ((), ()))
    tn = (((0,), (0,)), ((), ()))
    col = lax.broadcasted_iota(jnp.int32, (block, nb * block), 1) // block
    for i in range(nb):
        live = ((live_bits[h, i] >> col) & 1) == 1
        at = slice(i * block, (i + 1) * block)
        scores = lax.dot_general(q[at], k, nt, preferred_element_type=F32) * scale
        scores = jnp.where(live, scores, -jnp.inf)
        expon = jnp.exp(scores - jnp.max(scores, axis=1, keepdims=True))
        probs = expon / jnp.sum(expon, axis=1, keepdims=True)
        dprob = lax.dot_general(gg[at], vv, nt, preferred_element_type=F32)
        delta = jnp.sum(probs * dprob, axis=1, keepdims=True)
        p_s[at, :] = probs.astype(BF16)
        d_s[at, :] = (probs * (dprob - delta) * scale).astype(BF16)
    d = d_s[...]
    grad[0] = jnp.dot(d, k, preferred_element_type=F32).astype(BF16)
    grad[1] = lax.dot_general(d, q, tn, preferred_element_type=F32).astype(BF16)
    grad_v[...] = lax.dot_general(p_s[...], gg, tn, preferred_element_type=F32).astype(BF16)


def scatter_kernel(
    n_f, n_s, chunk, xt_h, full_q, full_k, grad, gv, gx_out, gv_out, gw_out,
    xt, wbuf, xsend, xrecv, own, zrecv, fown, fzrecv, fxrecv, gx, gxr,
    x_s, x_r, z_s, z_r, fz_s, fz_r, fx_s, fx_r, sp_s, sp_r, work,
):
    depth, z, x, s = place(n_f)
    rows, cols = gw_out.shape[1], gw_out.shape[2]
    few = first_rows(rows)
    half = (rows - few) // 2
    t, width = gx_out.shape

    def w_copy(i, slot):
        at = pl.ds(pl.multiple_of(i * chunk, 128), chunk)
        return [
            pltpu.make_async_copy(src.at[at], wbuf.at[slot, w], work.at[1 + w, slot])
            for w, src in enumerate((full_q, full_k))
        ]

    load = pltpu.make_async_copy(xt_h, xt, work.at[0, 0])
    load.start()
    for copy in w_copy(0, 0):
        copy.start()

    def order(i):
        odd = i % 2
        return odd * (i // 2) + (1 - odd) * (depth - 1 - i // 2)

    def part(c):
        w = c // 2
        return w, pl.ds(pl.multiple_of((c % 2) * half, 16), half)

    def main_rows(c):
        return pl.ds(pl.multiple_of(few + (c % 2) * half, 16), half)

    def product(zz, xx, w, start, size):
        at = pl.ds(pl.multiple_of((zz * 2 + xx) * rows + start, 16), size)
        return jnp.dot(xt[at, :], grad[w], preferred_element_type=F32).astype(BF16)

    def term(zz, xx, c):
        return product(zz, xx, c // 2, few + (c % 2) * half, half)

    def early_z(zz, e, slot, target):
        return remote(
            fown.at[zz, e], fzrecv.at[slot, e], fz_s.at[zz, e], fz_r.at[slot, e],
            "fsdp", target * 2 + x,
        )

    def early_x(w):
        return remote(
            fown.at[z, 2 + w], fxrecv.at[w], fx_s.at[w], fx_r.at[w], "fsdp", z * 2 + 1 - x
        )

    def to_x(zz, c):
        w, at = part(c)
        return remote(
            xsend.at[zz, w, at], xrecv.at[zz, w, at], x_s.at[zz, c], x_r.at[zz, c],
            "fsdp", z * 2 + 1 - x,
        )

    def to_z(zz, c, slot, target):
        w, at = part(c)
        return remote(
            own.at[zz, w, at], zrecv.at[slot, w, at], z_s.at[zz, c], z_r.at[slot, c],
            "fsdp", target * 2 + x,
        )

    def gv_copy(k):
        j = (s + k) % n_s
        return remote(
            gv.at[pl.ds(pl.multiple_of(j * t, 16), t)],
            gv_out.at[:, pl.ds(pl.multiple_of(s * cols, 128), cols)],
            sp_s.at[0, k - 1], sp_r.at[0, k - 1], "sp", j,
        )

    def gx_copy(k):
        j = (s + k) % n_s
        return remote(
            gx.at[pl.ds(pl.multiple_of(j * t, 16), t)], gxr.at[k - 1],
            sp_s.at[1, k - 1], sp_r.at[1, k - 1], "sp", j,
        )

    gv_own = pltpu.make_async_copy(
        gv.at[pl.ds(pl.multiple_of(s * t, 16), t)],
        gv_out.at[:, pl.ds(pl.multiple_of(s * cols, 128), cols)],
        work.at[0, 1],
    )
    gv_own.start()
    greet(n_f, n_s)
    for k in range(1, n_s):
        gv_copy(k).start()
    load.wait()

    @pl.loop(0, depth * PARTS)
    def _(i):
        zz, c = order(i // PARTS), i % PARTS
        w, at = part(c)
        xsend[zz, w, at, :] = term(zz, 1 - x, c)
        to_x(zz, c).start()

    @pl.loop(0, depth * 4)
    def _(i):
        zz, e = order(i // 4), i % 4
        rel = e // 2
        fown[zz, e] = product(zz, x + rel * (1 - 2 * x), e % 2, 0, few)

        @pl.when((z == 0) & (zz > z))
        def _():
            early_z(zz, e, zz, z + 1).start()

        @pl.when((z == depth - 1) & (zz < z))
        def _():
            early_z(zz, e, jnp.where(zz == z - 1, depth, zz), z - 1).start()

    @pl.loop(0, depth * PARTS)
    def _(i):
        zz, c = i // PARTS, i % PARTS
        w, at = part(c)
        own[zz, w, at, :] = term(zz, x, c)

    @pl.loop(0, depth * 4)
    def _(i):
        zz, e = order(i // 4), i % 4
        more = ((zz > z) & (z > 0)) | ((zz < z) & (z < depth - 1))

        @pl.when(more)
        def _():
            early_z(zz, e, zz, z).wait_recv()
            fown[zz, e] = (fown[zz, e].astype(F32) + fzrecv[zz, e].astype(F32)).astype(BF16)

        @pl.when((z > 0) & (zz > z))
        def _():
            early_z(zz, e, zz, z + 1).start()

        @pl.when((z < depth - 1) & (zz < z))
        def _():
            early_z(zz, e, jnp.where(zz == z - 1, depth, zz), z - 1).start()

    nt = (((1,), (1,)), ((), ()))
    chunks = width // chunk

    @pl.loop(0, chunks)
    def _(i):
        slot = i % 2
        for copy in w_copy(i, slot):
            copy.wait()

        @pl.when(i + 1 < chunks)
        def _():
            for copy in w_copy(i + 1, 1 - slot):
                copy.start()

        acc = lax.dot_general(grad[0], wbuf[slot, 0], nt, preferred_element_type=F32)
        acc += lax.dot_general(grad[1], wbuf[slot, 1], nt, preferred_element_type=F32)
        gx[:, pl.ds(pl.multiple_of(i * chunk, 128), chunk)] = acc.astype(BF16)

    for k in range(1, n_s):
        gx_copy(k).start()

    def early_sum(e):
        @pl.when(z > 0)
        def _():
            early_z(z, e, z, z).wait_recv()

        @pl.when(z < depth - 1)
        def _():
            early_z(z, e, depth, z).wait_recv()

        below = jnp.where(z > 0, fzrecv[z, e].astype(F32), 0.0)
        above = jnp.where(z < depth - 1, fzrecv[depth, e].astype(F32), 0.0)
        return fown[z, e].astype(F32) + below + above

    for w in range(2):
        fown[z, 2 + w] = early_sum(2 + w).astype(BF16)
        early_x(w).start()
    for w in range(2):
        gw_out[w, :few, :] = early_sum(w)

    @pl.loop(0, depth * PARTS)
    def _(i):
        zz, c = order(i // PARTS), i % PARTS
        w, at = part(c)
        to_x(zz, c).wait_recv()
        more = ((zz > z) & (z > 0)) | ((zz < z) & (z < depth - 1))

        def paired():
            return own[zz, w, at, :].astype(F32) + xrecv[zz, w, at, :].astype(F32)

        @pl.when(more)
        def _():
            to_z(zz, c, zz, z).wait_recv()
            own[zz, w, at, :] = (paired() + zrecv[zz, w, at, :].astype(F32)).astype(BF16)

        @pl.when(jnp.logical_not(more) & (zz != z))
        def _():
            own[zz, w, at, :] = paired().astype(BF16)

        @pl.when(zz > z)
        def _():
            to_z(zz, c, zz, z + 1).start()

        @pl.when(zz < z)
        def _():
            last = jnp.where(zz == z - 1, depth, zz)
            to_z(zz, c, last, z - 1).start()

        @pl.when(zz == z)
        def _():
            gw_out[w, main_rows(c), :] = paired()

    for w in range(2):
        early_x(w).wait_recv()
        gw_out[w, :few, :] += fxrecv[w].astype(F32)

    for k in range(1, n_s):
        gx_copy(k).wait_recv()

    @pl.loop(0, chunks)
    def _(i):
        at = pl.ds(pl.multiple_of(i * chunk, 128), chunk)
        acc = gx[pl.ds(pl.multiple_of(s * t, 16), t), at].astype(F32)
        for k in range(n_s - 1):
            acc += gxr[k, :, at].astype(F32)
        gx_out[:, at] = acc.astype(BF16)

    @pl.loop(0, PARTS)
    def _(c):
        w, at = part(c)

        @pl.when(z > 0)
        def _():
            to_z(z, c, z, z).wait_recv()
            gw_out[w, main_rows(c), :] += zrecv[z, w, at, :].astype(F32)

        @pl.when(z < depth - 1)
        def _():
            to_z(z, c, depth, z).wait_recv()
            gw_out[w, main_rows(c), :] += zrecv[depth, w, at, :].astype(F32)

    @pl.loop(0, depth * PARTS)
    def _(i):
        zz, c = i // PARTS, i % PARTS
        to_x(zz, c).wait_send()

        @pl.when(zz != z)
        def _():
            to_z(zz, c, zz, z).wait_send()
            early_z(zz, c, zz, z).wait_send()

    for w in range(2):
        early_x(w).wait_send()

    for k in range(1, n_s):
        gx_copy(k).wait_send()
        gv_copy(k).wait()
    gv_own.wait()


def local(n_f, n_s, tokens, w_query, w_key, values, grad_out, kv_index, kv_count):
    t, width = tokens.shape[1:]
    rows, cols = w_query.shape
    length = t * n_s
    heads = cols // HEAD_DIM
    depth = n_f // 2
    hbm = pl.BlockSpec(memory_space=pl.ANY)
    vmem = pl.BlockSpec(memory_space=pltpu.VMEM)
    smem = pl.BlockSpec(memory_space=pltpu.SMEM)
    dma = pltpu.SemaphoreType.DMA
    shape = jax.ShapeDtypeStruct
    slots = PARTS + 4
    q, k, full_q, full_k, full_v, full_g, xt = pl.pallas_call(
        functools.partial(gather_kernel, n_f, n_s),
        out_shape=(
            shape((length, cols), BF16),
            shape((length, cols), BF16),
            shape((width, cols), BF16),
            shape((width, cols), BF16),
            shape((length, cols), BF16),
            shape((length, cols), BF16),
            shape((width, length), BF16),
        ),
        in_specs=[hbm] * 5,
        out_specs=(vmem, vmem) + (hbm,) * 5,
        scratch_shapes=[
            pltpu.VMEM((length, width), BF16),
            pltpu.VMEM((width, length), BF16),
            pltpu.VMEM((2, width, cols), BF16),
            pltpu.VMEM((2, length, cols), F32),
            dma((depth, slots)),
            dma((depth, slots)),
            dma((depth, slots)),
            dma((depth, PARTS)),
            dma((depth, PARTS)),
            dma((2,)),
            dma((2,)),
            dma((n_s - 1,)),
            dma((n_s,)),
            dma((2, n_s - 1)),
            dma((2, n_s - 1)),
            dma((5,)),
            dma((n_f, 2)),
            dma((1,)),
        ],
        compiler_params=pltpu.CompilerParams(
            collective_id=0, has_side_effects=True, vmem_limit_bytes=60 * 2**20
        ),
        name="gather",
    )(tokens[0], w_query, w_key, values[0], grad_out[0])

    index, count = kv_index[0], kv_count[0]
    in_use = jnp.arange(index.shape[-1], dtype=jnp.int32) < count[..., None]
    live_bits = jnp.sum(jnp.where(in_use, 1 << index, 0), axis=-1, dtype=jnp.int32)
    head = pl.BlockSpec((length, HEAD_DIM), lambda h: (0, h))
    grad, gv = pl.pallas_call(
        attend_kernel,
        grid=(heads,),
        out_shape=(shape((2, length, cols), BF16), shape((length, cols), BF16)),
        in_specs=[smem, head, head, head, head],
        out_specs=(pl.BlockSpec((2, length, HEAD_DIM), lambda h: (0, 0, h)), head),
        scratch_shapes=[pltpu.VMEM((length, length), BF16), pltpu.VMEM((length, length), BF16)],
        compiler_params=pltpu.CompilerParams(vmem_limit_bytes=60 * 2**20),
        name="attend",
    )(live_bits, q, k, full_v, full_g)

    few = first_rows(rows)
    chunk = 512 if width % 512 == 0 else 128
    gx, token_gv, gw = pl.pallas_call(
        functools.partial(scatter_kernel, n_f, n_s, chunk),
        out_shape=(
            shape((t, width), BF16),
            shape((t, cols * n_s), BF16),
            shape((2, rows, cols), F32),
        ),
        in_specs=[hbm, hbm, hbm, vmem, vmem],
        out_specs=(vmem, hbm, vmem),
        scratch_shapes=[
            pltpu.VMEM((width, length), BF16),
            pltpu.VMEM((2, 2, chunk, cols), BF16),
            pltpu.VMEM((depth, 2, rows - few, cols), BF16),
            pltpu.VMEM((depth, 2, rows - few, cols), BF16),
            pltpu.VMEM((depth, 2, rows - few, cols), BF16),
            pltpu.VMEM((depth + 1, 2, rows - few, cols), BF16),
            pltpu.VMEM((depth, 4, few, cols), BF16),
            pltpu.VMEM((depth + 1, 4, few, cols), BF16),
            pltpu.VMEM((2, few, cols), BF16),
            pltpu.VMEM((length, width), BF16),
            pltpu.VMEM((n_s - 1, t, width), BF16),
            dma((depth, PARTS)),
            dma((depth, PARTS)),
            dma((depth, PARTS)),
            dma((depth + 1, PARTS)),
            dma((depth, 4)),
            dma((depth + 1, 4)),
            dma((2,)),
            dma((2,)),
            dma((2, n_s - 1)),
            dma((2, n_s - 1)),
            dma((3, 2)),
        ],
        compiler_params=pltpu.CompilerParams(
            collective_id=1, has_side_effects=True, vmem_limit_bytes=60 * 2**20
        ),
        name="scatter",
    )(xt, full_q, full_k, grad, gv)
    return (gx[None], token_gv[None], gw[0], gw[1])


def solution(mesh):
    in_specs = (
        P("fsdp", "sp", None),
        P("fsdp", "sp"),
        P("fsdp", "sp"),
        P("fsdp", "sp", None),
        P("fsdp", "sp", None),
        P("fsdp", "sp", None, None),
        P("fsdp", "sp", None),
    )
    out_specs = (P("fsdp", "sp", None), P("fsdp", "sp", None), P("fsdp", "sp"), P("fsdp", "sp"))
    return jax.shard_map(
        functools.partial(local, mesh.shape["fsdp"], mesh.shape["sp"]),
        mesh=mesh,
        in_specs=in_specs,
        out_specs=out_specs,
        check_vma=False,
    )
```
